512 devices in a mesh: dp: 64 (over z, y), mp: 8 (over x, core).
Axes of the slice: x: 4, y: 8, z: 8, core: 2. Of those that a mesh axis runs over, the one named last changes fastest.
Arguments:
- spikes: bfloat16 [3584, 16, 384], P('dp'), may hold values from -6 to 6
- session_ids: int32 [3584, 1], P('dp'), may hold values from 0 to 63; in each aligned block of 56 rows (0 to 55, 56 to 111, ...) at most 2 rows name the same one
- readin: bfloat16 [64, 384, 4096], P('dp', None, 'mp')
- gain: float32 [4096], P('mp'), may hold values from 0.5 to 1.5
- proj: bfloat16 [4096, 2048], P('mp', 'dp'), may hold values from -0.09375 to 0.09375
- query_bias: float32 [2048], P('mp'), may hold values from -1.5 to 1.5
- cotangent: bfloat16 [3584, 16, 2048], P('dp', None, 'mp'), may hold values from -0.0234375 to 0.0234375
Outputs:
- readin_grad: float32 [64, 384, 4096], P('dp', None, 'mp')
- gain_grad: float32 [4096], P('mp')
- proj_grad: float32 [4096, 2048], P('mp', 'dp')
The draws below stay inside these ranges and needn't reach their ends.
Inputs may be any that keep to these rules, and one draw needn't show every extreme that they name: `session_ids`: among the 56 windows of one device no session appears more than 2 times, and some session appears exactly 2 times.
All inputs are finite; a program needn't handle non-finite values.
Results may differ from the reference program's by a relative error of at most 0.011.
Values may be sent and summed in bfloat16 or wider, within the bound.
A program may use at most 64 MiB of HBM per device.

```python
import math
import jax
import jax.numpy as jnp
import numpy as np
from jax import lax

D = 4096
CH = 384
HEADS = 16
HD = 128
BINS = 16
MOST = 2
WIN_DEV = 56
WINDOWS = 3584
TOKENS = 57344
SESS = 64
HW = 2048
N_MP = 8


def draw_readin(key, part):
    key = jax.random.fold_in(key, 11)
    entry_key, column_key = jax.random.split(key)
    rise = 10.0
    base = jnp.clip(jax.random.normal(entry_key, (SESS, CH, D), jnp.float32), -6.0, 6.0)
    place = jnp.arange(D).astype(jnp.float32) / (D - 1)
    profile = jnp.exp(math.log(rise) * place)
    spread = math.sqrt((rise * rise - 1.0) / (2.0 * math.log(rise)))
    rough = jax.random.uniform(column_key, (D,), jnp.float32, 0.7, 1.3)
    values = base * (profile * rough / spread / math.sqrt(CH))
    return values.astype(jnp.bfloat16)


def steps_of(stream_key, extent, pieces, least, high):
    def one(position, parts):
        steps = jax.random.uniform(jax.random.fold_in(jax.random.fold_in(stream_key, 6), position), (parts,), jnp.float32, least / len(pieces), high / len(pieces))
        return jnp.repeat(jnp.exp(steps), extent[position] // parts).reshape((-1,) + (1,) * (len(extent) - position - 1))

    level = one(*pieces[0])
    for cut in pieces[1:]:
        level = level * one(*cut)
    return level


def routed_block(key, own, number, rows, amount, top, bound, skew):
    ranking = jax.random.permutation(key, amount)
    packed, usual = shares(amount, rows * top, bound, skew, True), shares(amount, rows * top, bound, skew, False)
    places = jnp.arange(amount)

    def named(sizes, turn):
        used = int((sizes > 0).sum())
        fixed = max(1, used // 4)
        shifted = fixed + (places - fixed + turn * (used - fixed)) % max(1, amount - fixed)
        return jnp.zeros((amount,), jnp.int32).at[ranking[jnp.where(places < fixed, places, shifted)]].set(jnp.asarray(sizes, jnp.int32))

    sizes = jnp.where(number % 4 == 0, named(packed, number // 4), named(usual, number - number // 4 - 1))
    mixed = jax.random.permutation(jax.random.fold_in(own, 3), amount)
    giver, sink = mixed[0:amount // 2 * 2:2], mixed[1:amount // 2 * 2:2]
    room = jnp.minimum(sizes[giver] - 1, bound - sizes[sink]) // 2
    room = jnp.where((giver == ranking[0]) | (sink == ranking[0]) | (sizes[sink] == 0), 0, jnp.maximum(room, 0))
    shifted = jax.random.randint(jax.random.fold_in(own, 4), (amount // 2,), 0, 1 << 20) % (room + 1)
    sizes = sizes.at[giver].add(-shifted).at[sink].add(shifted)
    items = jnp.searchsorted(jnp.cumsum(sizes), jnp.arange(rows * top), side="right").astype(jnp.int32)
    grid = items.reshape(top, rows).T
    grid = grid[jax.random.permutation(jax.random.fold_in(own, 1), rows)]
    turn = jax.random.randint(jax.random.fold_in(own, 2), (rows, 1), 0, top)
    return jnp.take_along_axis(grid, (jnp.arange(top)[None, :] + turn) % top, axis=1)


def shares(amount, total, reach, slope, full):
    weights = [(1 << 20) // math.isqrt(standing ** slope) + 1 for standing in range(1, amount + 1)]
    largest = reach if full else min(reach, max(-(-total // amount), total * weights[0] // sum(weights)))
    least = 1 if total - largest >= amount - 1 else 0
    counts, surplus = [largest] + [least] * (amount - 1), total - largest - least * (amount - 1)
    while surplus > 0:
        candidates = [i for i in range(1, amount) if counts[i] < largest] or [i for i in range(1, amount) if counts[i] < reach]
        whole, budget = sum([weights[i] for i in candidates]), surplus
        for i in candidates:
            more = min(reach - counts[i], max(1, budget * weights[i] // whole), surplus)
            counts[i] = counts[i] + more
            surplus = surplus - more
    return np.array(counts)


def centred(rng, shape, deviation, reach, shards=(), held_as=jnp.bfloat16):
    entries = deviation * jax.random.normal(rng, shape, jnp.float32)
    if shards:
        entries = entries * steps_of(rng, shape, shards, -0.22, 0.18)
    return jnp.clip(entries, -reach, reach).astype(held_as)


def setup_inputs(seed: int = 0) -> dict:
    key_list = jax.random.split(jax.random.key(seed), 8)
    spikes = centred(key_list[0], (WINDOWS, BINS, CH), 1.0, 6.0, ((0, 64),))
    session_ids_keys = jax.random.split(jax.random.fold_in(key_list[1], 1), WINDOWS // WIN_DEV)
    session_ids_turns = jax.random.permutation(jax.random.fold_in(key_list[1], 3), WINDOWS // WIN_DEV)
    session_ids = jax.vmap(lambda own, number: routed_block(jax.random.fold_in(key_list[1], 2), own, number, WIN_DEV, SESS, 1, MOST, 2))(session_ids_keys, session_ids_turns).reshape((WINDOWS, 1))
    readin = draw_readin(jax.random.fold_in(key_list[7], 71), 0)
    gain = jnp.clip(1.0 + 0.1 * jax.random.normal(key_list[3], (D,), jnp.float32), 0.5, 1.5)
    proj = centred(key_list[4], (D, HW), D ** -0.5, 0.09375, ((0, 8), (1, 64)))
    query_bias = jnp.clip(jax.random.uniform(key_list[5], (HW,), jnp.float32, -1.5, 1.5) * steps_of(key_list[5], (HW,), ((0, 8),), -0.4, 0.0), -1.5, 1.5)
    cotangent = centred(key_list[6], (WINDOWS, BINS, HW), TOKENS ** -0.5, 0.0234375, ((0, 64), (2, 8)))
    return dict(spikes=spikes, session_ids=session_ids, readin=readin, gain=gain, proj=proj, query_bias=query_bias, cotangent=cotangent)


eps_norm = 1e-05

def reference(spikes, session_ids, readin, gain, proj, query_bias, cotangent):
    sessions = session_ids[:, 0].astype(jnp.int32)

    def one_window(pair):
        window, which = pair
        table = lax.dynamic_index_in_dim(readin, which, 0, keepdims=False)
        return jnp.dot(window, table, preferred_element_type=jnp.float32).astype(jnp.bfloat16)
    features = lax.map(one_window, (spikes, sessions))
    features = features.reshape(TOKENS, D).astype(jnp.float32)
    inverse = lax.rsqrt(lax.optimization_barrier(jnp.mean(features * features, axis=-1, keepdims=True)) + eps_norm)
    normed = (features * inverse * gain).astype(jnp.bfloat16)
    block_width = D // N_MP
    queries = jnp.zeros((TOKENS, HW), jnp.float32)
    for member in range(N_MP):
        lower = member * block_width
        partial_block = jnp.dot(normed[:, lower:lower + block_width], proj[lower:lower + block_width], preferred_element_type=jnp.float32)
        partial_block = lax.optimization_barrier(partial_block.astype(jnp.bfloat16))
        queries = queries + partial_block.astype(jnp.float32)
    queries = queries + query_bias
    queries = queries.reshape(TOKENS, HEADS, HD)
    scale = lax.rsqrt(lax.optimization_barrier(jnp.mean(queries * queries, axis=-1, keepdims=True)) + eps_norm)
    unit = queries * scale
    upstream = cotangent.reshape(TOKENS, HEADS, HD).astype(jnp.float32)
    query_grad = scale * (upstream - unit * lax.optimization_barrier(jnp.mean(upstream * unit, axis=-1, keepdims=True)))
    query_grad = query_grad.reshape(TOKENS, HW).astype(jnp.bfloat16)
    proj_grad = jnp.dot(normed.T, query_grad, preferred_element_type=jnp.float32)
    normed_grad = jnp.dot(query_grad, proj.T, preferred_element_type=jnp.float32)
    gain_grad = lax.optimization_barrier(jnp.sum(normed_grad * features * inverse, axis=0))
    scaled_grad = gain * normed_grad
    feature_grad = inverse * scaled_grad - features * inverse ** 3 * lax.optimization_barrier(jnp.mean(scaled_grad * features, axis=-1, keepdims=True))
    feature_grad = feature_grad.astype(jnp.bfloat16).reshape(WINDOWS, BINS, D)

    def add_window(total, triple):
        window, grads, which = triple
        term = jnp.dot(window.T, grads, preferred_element_type=jnp.float32)
        return (total.at[which].add(term), None)
    start_total = jnp.zeros((SESS, CH, D), jnp.float32)
    readin_grad, unused = lax.scan(add_window, start_total, (spikes, feature_grad, sessions))
    return (readin_grad, gain_grad, proj_grad)
```

```python
import jax
import jax.numpy as jnp
from jax import lax
from jax.sharding import PartitionSpec as P

D = 4096
HD = 128
MOST = 2

eps_norm = 1e-05
F32 = jnp.float32
BF16 = jnp.bfloat16


def on_device(spikes, session_ids, readin, gain, proj, query_bias, cotangent):
    windows, bin_count, channels = spikes.shape
    owner_count = lax.axis_size("dp")
    mp_count = lax.axis_size("mp")
    slot_count = owner_count * MOST
    slice_width = readin.shape[2]
    share = cotangent.shape[2]
    owners = session_ids[:, 0]
    positions = jnp.arange(windows)
    earlier = (owners[:, None] == owners[None, :]) & (positions[None, :] < positions[:, None])
    ranked = jnp.sum(earlier.astype(jnp.int32), axis=1)
    target = owners * MOST + ranked
    placing = (jnp.arange(slot_count)[:, None] == target[None, :]).astype(BF16)

    def to_owner(rows):
        width = rows.shape[2]
        out = jnp.dot(placing, rows.reshape(windows, bin_count * width), preferred_element_type=F32)
        out = out.astype(BF16).reshape(owner_count, MOST * bin_count * width // 128, 128)
        out = lax.all_to_all(out, "dp", split_axis=0, concat_axis=0, tiled=True)
        return out.reshape(slot_count * bin_count, width)

    table = readin[0]
    scaled = (proj.astype(F32) * gain[:, None]).astype(BF16).T
    whole = lax.all_gather(scaled, "dp", axis=0, tiled=True)
    events = to_owner(spikes)
    upstream = to_owner(cotangent).astype(F32)
    maps = lax.dot_general(table, whole, (((1,), (1,)), ((), ())), preferred_element_type=F32)
    maps = maps.astype(BF16).reshape(channels, mp_count, share).transpose(1, 0, 2)
    maps = lax.all_to_all(maps, "mp", split_axis=0, concat_axis=0, tiled=True)
    maps = jnp.sum(maps.astype(F32), axis=0).astype(BF16)
    features = jnp.dot(events, table, preferred_element_type=F32)
    squares = lax.psum(jnp.sum(features * features, axis=-1), "mp")
    inverse = lax.rsqrt(squares / D + eps_norm)[:, None]
    raw = jnp.dot(events, maps, preferred_element_type=F32)
    tokens = raw.shape[0]
    queries = (raw * inverse + query_bias).reshape(tokens, share // HD, HD)
    scale = lax.rsqrt(jnp.mean(queries * queries, axis=-1, keepdims=True) + eps_norm)
    unit = queries * scale
    up = upstream.reshape(tokens, share // HD, HD)
    grad = scale * (up - unit * jnp.mean(up * unit, axis=-1, keepdims=True))
    grad = grad.reshape(tokens, share)
    cross = lax.psum(jnp.sum(grad * raw, axis=-1), "mp")
    weight = inverse**3 * (cross / D)[:, None]
    moved = (grad * inverse).astype(BF16)
    across = lax.dot_general(moved, events, (((0,), (0,)), ((), ())), preferred_element_type=F32)
    across = lax.all_gather(across.astype(BF16), "mp", axis=0, tiled=True)
    part = jnp.dot(across, table, preferred_element_type=F32).astype(BF16)
    part = part.reshape(owner_count, proj.shape[1], slice_width)
    part = lax.all_to_all(part, "dp", split_axis=0, concat_axis=0, tiled=True)
    total = jnp.sum(part.astype(F32), axis=0).T
    gain_grad = lax.psum(jnp.sum(total * proj.astype(F32), axis=1), "dp")
    proj_grad = total * gain[:, None]
    inner = lax.dot_general(
        events, (events.astype(F32) * weight).astype(BF16), (((0,), (0,)), ((), ())), preferred_element_type=F32
    )
    readin_grad = lax.dot_general(across, whole, (((0,), (0,)), ((), ())), preferred_element_type=F32)
    readin_grad = readin_grad - jnp.dot(inner.astype(BF16), table, preferred_element_type=F32)
    return (readin_grad[None], gain_grad, proj_grad)


def solution(mesh):
    return jax.shard_map(
        on_device,
        mesh=mesh,
        in_specs=(
            P("dp", None, None),
            P("dp", None),
            P("dp", None, "mp"),
            P("mp"),
            P("mp", "dp"),
            P("mp"),
            P("dp", None, "mp"),
        ),
        out_specs=(P("dp", None, "mp"), P("mp"), P("mp", "dp")),
        check_vma=False,
    )
```
